32 devices in a mesh: groups: 2 (over y), rep: 4 (over z), tp: 4 (over x, core).
Axes of the slice: x: 2, y: 2, z: 4, core: 2. Of those that a mesh axis runs over, the one named last changes fastest.
Arguments:
- tokens_in: bfloat16 [16384, 8192], P(('groups', 'rep'), 'tp'), parts along dimension 0, may hold values from -6 to 6
- upstream: bfloat16 [16384, 1024], P(('groups', 'rep')), parts along dimension 0, may hold values from -6 to 6
- base_weight: bfloat16 [8192, 1024], P('tp'), may hold values from -0.1875 to 0.1875
- bank_a: bfloat16 [32, 16, 8192], P('rep', None, 'tp'), may hold values from -0.125 to 0.125
- bank_b: bfloat16 [32, 16, 1024], P('rep', None, 'tp'), may hold values from -0.1875 to 0.1875
- slot_ids: int32 [16384], P(('groups', 'rep')), parts along dimension 0, may hold values from 0 to 7, as said below
- used_lists: int32 [8, 8], P(('groups', 'rep')), parts along dimension 0, may hold values from 0 to 31, as said below
Outputs:
- token_gradient: bfloat16 [16384, 8192], P(('groups', 'rep'), 'tp'), parts along dimension 0
- grad_a: float32 [64, 16, 8192], P(('groups', 'rep'), None, 'tp'), parts along dimension 0
- grad_b: float32 [64, 16, 1024], P(('groups', 'rep'), None, 'tp'), parts along dimension 0
The draws below stay inside these ranges and needn't reach their ends.
There are 2 independent parts, one for each index of `groups`. The reference program is written for one: setup_inputs(seed, part) draws one part's arguments, and reference() takes and returns one part's arrays. A program takes and returns all parts, laid end to end along the dimension named above; an argument that names none is the same for every part. Nothing has to cross between parts.
Inputs may be any that keep to these rules, and one draw needn't show every extreme that they name: `slot_ids`: constant within aligned blocks of 128 rows, never falling within one replica's 2048 rows, and every value 0 to 7 appears in every replica. `used_lists`: A replica's 8 ids are distinct; replica o owns ids o * 8 to (o + 1) * 8 - 1, and at most 2 ids of one list have the same owner, exactly 2 for some owner in every list.
All inputs are finite; a program needn't handle non-finite values.
Results may differ from the reference program's by a relative error of at most 0.0034.
Values may be sent and summed in bfloat16 or wider, within the bound.
No kernel may reach another device: no remote copies, remote signals or barrier semaphores. Data moves between devices by JAX's collectives and lax.ppermute only.
A program may use at most 128 MiB of HBM per device.

```python
import jax
import jax.numpy as jnp
from jax import lax

D = 8192
F = 1024
R = 16
BLOCK = 128
TOK_DEV = 2048
ADP_DEV = 8
SLOTS = 8
CAP = 2
TOKENS = 8192
ADAPTERS = 32
N_REP = 4


def draw_slot_ids(key, part):
    key = jax.random.fold_in(key, 11)
    block_count = TOK_DEV // BLOCK

    def one_replica(subkey):
        shuffled = jax.random.permutation(subkey, jnp.arange(1, block_count, dtype=jnp.int32))
        cuts = jnp.sort(shuffled[:SLOTS - 1])
        blocks = jnp.arange(block_count, dtype=jnp.int32)
        block_slot = jnp.sum((blocks[:, None] >= cuts[None, :]).astype(jnp.int32), axis=1)
        return jnp.repeat(block_slot, BLOCK).astype(jnp.int32)
    return jax.vmap(one_replica)(jax.random.split(key, N_REP)).reshape(-1).astype(jnp.int32)


def draw_used_lists(key, part):
    key = jax.random.fold_in(key, 23)
    owner_count = SLOTS // CAP

    def pick_local(subkey):
        return jax.random.permutation(subkey, jnp.arange(ADP_DEV, dtype=jnp.int32))[:CAP]

    def one_replica(subkey):
        first, second, third = jax.random.split(subkey, 3)
        owners = jax.random.permutation(first, jnp.arange(N_REP, dtype=jnp.int32))[:owner_count]
        local_ids = jax.vmap(pick_local)(jax.random.split(second, owner_count))
        listed = (owners[:, None] * ADP_DEV + local_ids).reshape(SLOTS)
        order = jax.random.permutation(third, jnp.arange(SLOTS, dtype=jnp.int32))
        return listed[order].astype(jnp.int32)
    return jax.vmap(one_replica)(jax.random.split(key, N_REP)).astype(jnp.int32)


def levels(rng, extent, cuts, smallest, high):
    loudness = 1.0
    for position, parts in cuts:
        draws = jax.random.uniform(jax.random.fold_in(jax.random.fold_in(rng, 6), position), (parts,), jnp.float32, smallest / len(cuts), high / len(cuts))
        loudness = loudness * jnp.repeat(jnp.exp(draws), extent[position] // parts).reshape((-1,) + (1,) * (len(extent) - 1 - position))
    return loudness


def noise(key, dims, deviation, limit, pieces=(), kind=jnp.bfloat16):
    values = jax.random.normal(key, dims, jnp.float32) * deviation
    if len(pieces) > 0:
        values = levels(key, dims, pieces, -0.22, 0.18) * values
    return jnp.clip(values, min=-limit, max=limit).astype(kind)


def setup_inputs(seed: int = 0, part: int = 0) -> dict:
    seeds = jax.random.split(jax.random.key(seed), 8)
    part_keys = jax.random.split(jax.random.fold_in(seeds[7], part), 8)
    return {
        "tokens_in": noise(part_keys[0], (TOKENS, D), 1.0, 6.0, ((0, 4), (1, 4))),
        "upstream": noise(part_keys[1], (TOKENS, F), 1.0, 6.0, ((0, 4),)),
        "base_weight": noise(seeds[2], (D, F), F ** -0.5, 0.1875, ((0, 4),)),
        "bank_a": noise(seeds[3], (ADAPTERS, R, D), (D // 4) ** -0.5, 0.125, ((0, 4), (2, 4))),
        "bank_b": noise(seeds[4], (ADAPTERS, R, F), F ** -0.5, 0.1875, ((0, 4), (2, 4))),
        "slot_ids": draw_slot_ids(jax.random.fold_in(jax.random.fold_in(seeds[7], part), 71), part),
        "used_lists": draw_used_lists(jax.random.fold_in(jax.random.fold_in(seeds[7], part), 71), part),
    }


adapter_scale = 2.0


def reference(tokens_in, upstream, base_weight, bank_a, bank_b, slot_ids, used_lists):
    block_total = TOKENS // BLOCK
    block_slot = slot_ids.reshape(block_total, BLOCK)[:, 0].astype(jnp.int32)
    block_owner = (jnp.arange(block_total) // (TOK_DEV // BLOCK)).astype(jnp.int32)
    block_adapter = used_lists[block_owner, block_slot].astype(jnp.int32)
    token_blocks = tokens_in.reshape(block_total, BLOCK, D)
    grad_blocks = upstream.reshape(block_total, BLOCK, F)

    def one_block(items):
        rows_x, rows_g, which = items
        down_matrix = bank_a[which]
        up_mat = bank_b[which]
        down_weight = jnp.dot(rows_x, down_matrix.T, preferred_element_type=jnp.float32)
        up_weight = jnp.dot(rows_g, up_mat.T, preferred_element_type=jnp.float32)
        scaled_down_weight = (adapter_scale * down_weight).astype(jnp.bfloat16)
        scaled_up_weight = (adapter_scale * up_weight).astype(jnp.bfloat16)
        frozen_value_term = jnp.dot(rows_g, base_weight.T, preferred_element_type=jnp.float32)
        adapter_term = jnp.dot(scaled_up_weight, down_matrix, preferred_element_type=jnp.float32)
        gradient_row_block = (frozen_value_term + adapter_term).astype(jnp.bfloat16)
        block_ga = jnp.dot(scaled_up_weight.T, rows_x, preferred_element_type=jnp.float32)
        block_gb = jnp.dot(scaled_down_weight.T, rows_g, preferred_element_type=jnp.float32)
        return gradient_row_block, block_ga, block_gb

    gradient_row_block, block_ga, block_gb = lax.map(one_block, (token_blocks, grad_blocks, block_adapter))
    token_gradient = gradient_row_block.reshape(TOKENS, D)
    grad_a = jnp.zeros((ADAPTERS, R, D), jnp.float32).at[block_adapter].add(block_ga)
    grad_b = jnp.zeros((ADAPTERS, R, F), jnp.float32).at[block_adapter].add(block_gb)
    return token_gradient, grad_a, grad_b
```

```python
import functools

import jax
import jax.numpy as jnp
from jax import lax
from jax.experimental import pallas as pl
from jax.experimental.pallas import tpu as pltpu
from jax.sharding import PartitionSpec as P

BLOCK = 128
SCALE = 2.0
VMEM_LIMIT = 48 * 1024 * 1024

F32 = jnp.float32
BF16 = jnp.bfloat16
ANY = pl.BlockSpec(memory_space=pl.ANY)
SMEM = pl.BlockSpec(memory_space=pltpu.SMEM)
VMEM = pl.BlockSpec(memory_space=pltpu.VMEM)
NT = (((1,), (1,)), ((), ()))
TN = (((0,), (0,)), ((), ()))


def params(**kw):
    return pltpu.CompilerParams(vmem_limit_bytes=VMEM_LIMIT, **kw)


def cost(flops, nbytes):
    return pl.CostEstimate(flops=int(flops), bytes_accessed=int(nbytes), transcendentals=0)


def whole(shape):
    return pl.BlockSpec(shape, lambda *_: (0,) * len(shape))


def owner_of(ident, held):
    return lax.div(ident, jnp.int32(held))


def pick_kernel(rep, cap, held, slots, nb, *refs):
    lists = refs[:rep]
    slot_ids, bank_a = refs[rep : rep + 2]
    outs = refs[rep + 2 : rep + 2 + rep]
    pick, sel, vslot = refs[2 * rep + 2 : 2 * rep + 5]
    place_v, sems = refs[2 * rep + 5 :]
    me = lax.axis_index("rep")
    for s in range(rep):
        count = jnp.int32(0)
        idx = [jnp.int32(-1)] * cap
        for k in range(slots):
            ident = lists[s][0, k]
            mine = owner_of(ident, held) == me
            for c in range(cap):
                idx[c] = jnp.where(mine & (count == c), lax.rem(ident, jnp.int32(held)), idx[c])
            count = count + mine.astype(jnp.int32)
        for c in range(cap):
            pick[s * cap + c] = idx[c]
            pltpu.make_async_copy(
                bank_a.at[jnp.maximum(idx[c], 0)], outs[s].at[c], sems.at[s, c]
            ).start()
    ids = [lists[0][0, k] for k in range(slots)]
    owners = [owner_of(i, held) for i in ids]
    for v in range(rep * cap):
        sel[v] = jnp.int32(0)
    for k in range(slots):
        place = jnp.int32(0)
        for j in range(k):
            place = place + (owners[j] == owners[k]).astype(jnp.int32)
        v = jnp.bitwise_xor(owners[k], me) * cap + place
        place_v[k] = v
        sel[v] = lax.rem(ids[k], jnp.int32(held))
    for b in range(nb):
        vslot[b] = place_v[slot_ids[b, 0]]
    for s in range(rep):
        for c in range(cap):
            pltpu.make_async_copy(bank_a.at[0], outs[s].at[c], sems.at[s, c]).wait()


def select_kernel(rep, cap, rank, *refs):
    sel = refs[0]
    banks = refs[1 : 1 + rep]
    out = refs[1 + rep]
    for v in range(rep * cap):
        start = pl.multiple_of(sel[v] * rank, rank)
        out[v * rank : (v + 1) * rank, :] = banks[v // cap][pl.ds(start, rank), :]


def up_kernel(rep, cap, rank, tp, nb, *refs):
    vslot, upstream = refs[:2]
    quarters = refs[2 : 2 + tp]
    tokens = refs[2 + tp]
    up_out = refs[3 + tp]
    grads = refs[4 + tp :]
    width = rep * cap * rank
    per = cap * rank
    cols = quarters[0].shape[1]
    tp_rank = lax.axis_index("tp")

    @pl.when(pl.program_id(0) == 0)
    def _():
        chunk = 4
        lane_slot = lax.broadcasted_iota(jnp.int32, (BLOCK, width), 1) // rank
        for r in range(nb // chunk):
            rows = slice(r * chunk * BLOCK, (r + 1) * chunk * BLOCK)
            acc = None
            for s in range(tp):
                at = pl.multiple_of(jnp.bitwise_xor(tp_rank, s) * cols, cols)
                part = lax.dot_general(
                    upstream[rows, pl.ds(at, cols)], quarters[s][...], NT, preferred_element_type=F32
                )
                acc = part if acc is None else acc + part
            acc = (SCALE * acc).astype(BF16)
            for b in range(chunk):
                blk = r * chunk + b
                keep = lane_slot == vslot[blk]
                part = acc[b * BLOCK : (b + 1) * BLOCK, :]
                up_out[blk * BLOCK : (blk + 1) * BLOCK, :] = jnp.where(keep, part, jnp.zeros_like(part))

    grad = lax.dot_general(up_out[...], tokens[...], TN, preferred_element_type=F32)
    for s in range(rep):
        grads[s][...] = grad[s * per : (s + 1) * per, :].astype(grads[s].dtype)


def down_kernel(rep, cap, rank, blocks, *refs):
    vslot, tokens = refs[:2]
    parts = refs[2 : 2 + rep]
    down, a_all = refs[2 + rep : 4 + rep]
    turned = refs[4 + rep]
    per = cap * rank
    step = pl.program_id(0)

    @pl.when(step == 0)
    def _():
        for s in range(rep):
            a_all[s * per : (s + 1) * per, :] = parts[s][...]

    prod = lax.dot_general(tokens[...], a_all[...], NT, preferred_element_type=F32)
    for b in range(blocks):
        turned[b] = prod[b * BLOCK : (b + 1) * BLOCK, :].T
    for b in range(blocks):
        start = pl.multiple_of(vslot[step * blocks + b] * rank, rank)
        down[:, b * BLOCK : (b + 1) * BLOCK] = turned[b, pl.ds(start, rank), :]


def grad_b_kernel(rep, cap, rank, nb, *refs):
    vslot, down_here, down_there, upstream = refs[:4]
    grads = refs[4 : 4 + rep]
    spread, mine, sem = refs[4 + rep :]
    per = cap * rank
    cols = mine.shape[1]
    at = pl.multiple_of(lax.axis_index("tp") * cols, cols)
    copy = pltpu.make_async_copy(upstream.at[:, pl.ds(at, cols)], mine, sem)
    copy.start()
    spread[...] = jnp.zeros_like(spread)
    total = (SCALE * (down_here[...] + down_there[...])).astype(BF16)
    for b in range(nb):
        start = pl.multiple_of(vslot[b] * rank, rank)
        spread[pl.ds(start, rank), b * BLOCK : (b + 1) * BLOCK] = total[:, b * BLOCK : (b + 1) * BLOCK]
    copy.wait()
    grad = jnp.dot(spread[...], mine[...], preferred_element_type=F32)
    for s in range(rep):
        grads[s][...] = grad[s * per : (s + 1) * per, :].astype(grads[s].dtype)


def token_kernel(aliased, chunk, *refs):
    upstream, up_scaled, weight, a_all = refs[:4]
    out = refs[-1]
    rows = upstream.shape[0]
    for r in range(rows // chunk):
        at = slice(r * chunk, (r + 1) * chunk)
        frozen = lax.dot_general(upstream[at, :], weight[...], NT, preferred_element_type=F32)
        low = jnp.dot(up_scaled[at, :], a_all[...], preferred_element_type=F32)
        out[at, :] = (frozen + low).astype(BF16)


def token_part(upstream, up_scaled, weight, a_all, tile, first, count, before=None):
    rows, outs = upstream.shape
    width = weight.shape[0]
    depth = a_all.shape[0]
    args = [upstream, up_scaled, weight, a_all]
    specs = [
        whole((rows, outs)),
        whole((rows, depth)),
        pl.BlockSpec((tile, outs), lambda i: (i + first, 0)),
        pl.BlockSpec((depth, tile), lambda i: (0, i + first)),
    ]
    alias = {}
    if before is not None:
        args.append(before)
        specs.append(ANY)
        alias = {4: 0}
    return pl.pallas_call(
        functools.partial(token_kernel, before is not None, 512),
        out_shape=jax.ShapeDtypeStruct((rows, width), BF16),
        grid=(count,),
        in_specs=specs,
        out_specs=pl.BlockSpec((rows, tile), lambda i: (0, i + first)),
        input_output_aliases=alias,
        compiler_params=params(),
        cost_estimate=cost(2 * rows * (outs + 256) * tile * count, 2 * rows * (outs + tile * count)),
        name="token_gradient",
    )(*args)


def finish_kernel(rep, cap, rank, *refs):
    pick = refs[0]
    in_a = refs[1 : 1 + rep]
    in_b = refs[1 + rep : 1 + 2 * rep]
    out_a, out_b = refs[1 + 2 * rep :]
    out_a[...] = jnp.zeros_like(out_a)
    out_b[...] = jnp.zeros_like(out_b)
    for s in range(rep):
        for c in range(cap):
            to = pick[s * cap + c]

            @pl.when(to >= 0)
            def _():
                out_a[to] += in_a[s][c * rank : (c + 1) * rank, :].astype(F32)
                out_b[to] += in_b[s][c * rank : (c + 1) * rank, :].astype(F32)


def local(tokens_in, upstream, base_weight, bank_a, bank_b, slot_ids, used_lists):
    rows, width = tokens_in.shape
    outs = upstream.shape[1]
    held, rank, cols = bank_b.shape
    slots = used_lists.shape[1]
    nb = rows // BLOCK
    rep = lax.axis_size("rep")
    tp = lax.axis_size("tp")
    cap = (slots + rep - 1) // rep
    per = cap * rank
    depth = rep * per

    def along(axis, size, x, s):
        return lax.ppermute(x, axis, [(i, i ^ s) for i in range(size)])

    def rep_swap(x, s):
        return along("rep", rep, x, s)

    def tp_swap(x, s):
        return along("tp", tp, x, s)

    struct = jax.ShapeDtypeStruct
    lists = [used_lists] + [rep_swap(used_lists, s) for s in range(1, rep)]
    b_flat = bank_b.reshape(held * rank, cols)
    banks = [b_flat] + [rep_swap(b_flat, s) for s in range(1, rep)]

    picked = pl.pallas_call(
        functools.partial(pick_kernel, rep, cap, held, slots, nb),
        out_shape=[struct((cap, rank, width), BF16)] * rep
        + [struct((rep * cap,), jnp.int32), struct((rep * cap,), jnp.int32), struct((nb,), jnp.int32)],
        in_specs=[SMEM] * (rep + 1) + [ANY],
        out_specs=[ANY] * rep + [SMEM] * 3,
        scratch_shapes=[pltpu.SMEM((slots,), jnp.int32), pltpu.SemaphoreType.DMA((rep, cap))],
        compiler_params=params(),
        cost_estimate=cost(0, 4 * depth * width),
        name="pick",
    )(*lists, slot_ids.reshape(nb, BLOCK), bank_a)
    send_a = [x.reshape(per, width) for x in picked[:rep]]
    pick, sel, vslot = picked[rep:]
    recv_a = [send_a[0]] + [rep_swap(send_a[s], s) for s in range(1, rep)]

    quarter = pl.pallas_call(
        functools.partial(select_kernel, rep, cap, rank),
        out_shape=struct((depth, cols), BF16),
        in_specs=[SMEM] + [VMEM] * rep,
        out_specs=VMEM,
        compiler_params=params(),
        cost_estimate=cost(0, 4 * depth * cols),
        name="select_b",
    )(sel, *banks)
    quarters = {0: quarter}
    bit = tp // 2
    while bit:
        quarters.update({s | bit: tp_swap(q, bit) for s, q in quarters.items()})
        bit //= 2

    tile = 512
    steps = width // tile
    up_scaled, *grads_a = pl.pallas_call(
        functools.partial(up_kernel, rep, cap, rank, tp, nb),
        out_shape=[struct((rows, depth), BF16), struct((per, width), F32)] + [struct((per, width), BF16)] * (rep - 1),
        grid=(steps,),
        in_specs=[SMEM, whole((rows, outs))]
        + [whole((depth, cols))] * tp
        + [pl.BlockSpec((rows, tile), lambda i: (0, i))],
        out_specs=[whole((rows, depth))] + [pl.BlockSpec((per, tile), lambda i: (0, i))] * rep,
        compiler_params=params(),
        cost_estimate=cost(2 * rows * depth * (width + outs), 2 * rows * (width + outs)),
        name="up_grad_a",
    )(vslot, upstream, *[quarters[s] for s in range(tp)], tokens_in)
    recv_ga = [grads_a[0]] + [rep_swap(grads_a[s], s) for s in range(1, rep)]

    blocks = 4
    down, a_all = pl.pallas_call(
        functools.partial(down_kernel, rep, cap, rank, blocks),
        out_shape=[struct((rank, rows), F32), struct((depth, width), BF16)],
        grid=(nb // blocks,),
        in_specs=[SMEM, pl.BlockSpec((blocks * BLOCK, width), lambda i: (i, 0))] + [whole((per, width))] * rep,
        out_specs=[pl.BlockSpec((rank, blocks * BLOCK), lambda i: (0, i)), whole((depth, width))],
        scratch_shapes=[pltpu.VMEM((blocks, depth, BLOCK), F32)],
        compiler_params=params(),
        cost_estimate=cost(2 * rows * depth * width, 2 * rows * width),
        name="down",
    )(vslot, tokens_in, *recv_a)
    bit = 1
    while 2 * bit < tp:
        down = down + tp_swap(down, bit)
        bit *= 2
    down_there = tp_swap(down, bit)

    half = steps // 2
    token_gradient = token_part(upstream, up_scaled, base_weight, a_all, tile, 0, half)
    token_gradient = token_part(upstream, up_scaled, base_weight, a_all, tile, half, steps - half, token_gradient)

    grads_b = pl.pallas_call(
        functools.partial(grad_b_kernel, rep, cap, rank, nb),
        out_shape=[struct((per, cols), F32)] + [struct((per, cols), F32)] * (rep - 1),
        in_specs=[SMEM, VMEM, VMEM, ANY],
        out_specs=[VMEM] * rep,
        scratch_shapes=[
            pltpu.VMEM((depth, rows), BF16),
            pltpu.VMEM((rows, cols), BF16),
            pltpu.SemaphoreType.DMA,
        ],
        compiler_params=params(),
        cost_estimate=cost(2 * rows * depth * cols, 2 * rows * cols),
        name="grad_b",
    )(vslot, down, down_there, upstream)
    recv_gb = [grads_b[0]] + [rep_swap(grads_b[s], s) for s in range(1, rep)]

    grad_a, grad_b = pl.pallas_call(
        functools.partial(finish_kernel, rep, cap, rank),
        out_shape=[struct((held, rank, width), F32), struct((held, rank, cols), F32)],
        in_specs=[SMEM] + [VMEM] * (2 * rep),
        out_specs=[VMEM] * 2,
        compiler_params=params(),
        cost_estimate=cost(0, 4 * held * rank * width),
        name="finish",
    )(pick, *recv_ga, *recv_gb)
    return token_gradient, grad_a, grad_b


def solution(mesh):
    in_specs = (
        P(("groups", "rep"), "tp"),
        P(("groups", "rep"), None),
        P("tp", None),
        P("rep", None, "tp"),
        P("rep", None, "tp"),
        P(("groups", "rep")),
        P(("groups", "rep"), None),
    )
    out_specs = (
        P(("groups", "rep"), "tp"),
        P(("groups", "rep"), None, "tp"),
        P(("groups", "rep"), None, "tp"),
    )
    return jax.shard_map(local, mesh=mesh, in_specs=in_specs, out_specs=out_specs, check_vma=False)
```

```python
import functools

import jax
import jax.numpy as jnp
from jax import lax
from jax.experimental import pallas as pl
from jax.experimental.pallas import tpu as pltpu
from jax.sharding import PartitionSpec as P

BLOCK = 128
SCALE = 2.0
VMEM_LIMIT = 12 * 1024 * 1024

F32 = jnp.float32
BF16 = jnp.bfloat16
I32 = jnp.int32
ANY = pl.BlockSpec(memory_space=pl.ANY)
HBM = pl.BlockSpec(memory_space=pltpu.HBM)
SMEM = pl.BlockSpec(memory_space=pltpu.SMEM)
VMEM = pl.BlockSpec(memory_space=pltpu.VMEM)
NT = (((1,), (1,)), ((), ()))
TN = (((0,), (0,)), ((), ()))
struct = jax.ShapeDtypeStruct


def in_hbm(x):
    return pltpu.with_memory_space_constraint(x, pltpu.HBM)


def kernel(body, name, outs, in_specs, out_specs, args, scratch=()):
    return pl.pallas_call(
        body,
        out_shape=outs,
        in_specs=in_specs,
        out_specs=out_specs,
        scratch_shapes=list(scratch),
        compiler_params=pltpu.CompilerParams(vmem_limit_bytes=VMEM_LIMIT),
        cost_estimate=pl.CostEstimate(flops=0, bytes_accessed=0, transcendentals=0),
        name=name,
    )(*args)


def start_all(copies):
    for copy in copies:
        copy.start()
    return copies


def wait_all(copies):
    for copy in copies:
        copy.wait()


def split(ident, held):
    if held & (held - 1) == 0:
        shift = held.bit_length() - 1
        return lax.shift_right_logical(ident, I32(shift)), jnp.bitwise_and(ident, I32(held - 1))
    return lax.div(ident, I32(held)), lax.rem(ident, I32(held))


def plan_kernel(cap, held, my_list, slot_ids, bank_a, bank_b, vslot, bank, lists, ids, place_v, sems):
    slots = lists.shape[1]
    width = bank_a.shape[1]
    copies = start_all(
        [
            pltpu.make_async_copy(my_list, lists, sems.at[0]),
            pltpu.make_async_copy(slot_ids, ids, sems.at[1]),
            pltpu.make_async_copy(bank_a, bank.at[:, pl.ds(0, width)], sems.at[2]),
            pltpu.make_async_copy(bank_b, bank.at[:, pl.ds(width, bank_b.shape[1])], sems.at[3]),
        ]
    )
    me = lax.axis_index("rep")
    copies[0].wait()
    owners = [split(lists[0, k], held)[0] for k in range(slots)]
    for k in range(slots):
        place = I32(0)
        for j in range(k):
            place = place + (owners[j] == owners[k]).astype(I32)
        place_v[k] = jnp.bitwise_xor(owners[k], me) * cap + place
    copies[1].wait()
    for b in range(vslot.shape[0]):
        vslot[b] = place_v[ids[b, 0]]
    wait_all(copies[2:])


def pick_kernel(rep, cap, held, *refs):
    sources = refs[:rep]
    bank = refs[rep]
    outs = refs[rep + 1 : 2 * rep + 1]
    pick = refs[2 * rep + 1]
    lists = refs[2 * rep + 2 : 3 * rep + 2]
    sems = refs[3 * rep + 2]
    rank = outs[0].shape[0] // cap
    slots = lists[0].shape[1]
    me = lax.axis_index("rep")
    loads = start_all([pltpu.make_async_copy(sources[s], lists[s], sems.at[s]) for s in range(rep)])
    wait_all(loads)
    for s in range(rep):
        count = I32(0)
        idx = [I32(-1)] * cap
        for k in range(slots):
            owner, number = split(lists[s][0, k], held)
            mine = owner == me
            for c in range(cap):
                idx[c] = jnp.where(mine & (count == c), number, idx[c])
            count = count + mine.astype(I32)
        for c in range(cap):
            pick[s * cap + c] = idx[c]
            start = pl.multiple_of(jnp.maximum(idx[c], 0) * rank, rank)
            outs[s][c * rank : (c + 1) * rank, :] = bank[pl.ds(start, rank), :]


def frozen_kernel(chunk, tile, upstream, weight, tokens, after, out, upstream_v, tokens_v, weight_v, sems):
    del after
    rows = upstream.shape[0]
    width = weight.shape[0]
    n_rows, n_cols = rows // chunk, width // tile

    def fetch(source, to, i, size, sem):
        at = pl.ds(i * size, size)
        return pltpu.make_async_copy(source.at[at, :], to.at[at, :], sems.at[sem])

    weights = [fetch(weight, weight_v, t, tile, t) for t in range(n_cols)]
    ups = [fetch(upstream, upstream_v, r, chunk, n_cols + r) for r in range(n_rows)]
    toks = [fetch(tokens, tokens_v, r, chunk, n_cols + n_rows + r) for r in range(n_rows)]
    start_all(weights[:1] + ups + weights[1:] + toks)
    for t in range(n_cols):
        weights[t].wait()
        cols = slice(t * tile, (t + 1) * tile)
        for r in range(n_rows):
            if t == 0:
                ups[r].wait()
            at = slice(r * chunk, (r + 1) * chunk)
            out[at, cols] = lax.dot_general(
                upstream_v[at, :], weight_v[cols, :], NT, preferred_element_type=F32
            )
    wait_all(toks)


def up_kernel(rep, cap, rank, nb, order, *refs):
    vslot, upstream, held_q, came_q, tokens = refs[:5]
    up_out = refs[6]
    grads = refs[7:]
    width = rep * cap * rank
    per = cap * rank
    cols = held_q.shape[1]
    tp_rank = lax.axis_index("tp")
    chunk = 4
    lane_slot = lax.broadcasted_iota(I32, (BLOCK, width), 1) // rank
    for r in range(nb // chunk):
        rows = slice(r * chunk * BLOCK, (r + 1) * chunk * BLOCK)
        acc = None
        for i, s in enumerate(order):
            for j, piece in ((0, held_q), (1, came_q)):
                at = pl.multiple_of(jnp.bitwise_xor(tp_rank, s ^ j) * cols, cols)
                part = lax.dot_general(
                    upstream[rows, pl.ds(at, cols)],
                    piece[i * width : (i + 1) * width, :],
                    NT,
                    preferred_element_type=F32,
                )
                acc = part if acc is None else acc + part
        acc = (SCALE * acc).astype(BF16)
        for b in range(chunk):
            blk = r * chunk + b
            part = acc[b * BLOCK : (b + 1) * BLOCK, :]
            up_out[blk * BLOCK : (blk + 1) * BLOCK, :] = jnp.where(
                lane_slot == vslot[blk], part, jnp.zeros_like(part)
            )
    tile = 512
    for t in range(tokens.shape[1] // tile):
        at = slice(t * tile, (t + 1) * tile)
        grad = lax.dot_general(up_out[...], tokens[:, at], TN, preferred_element_type=F32)
        for s in range(rep):
            grads[s][:, at] = grad[s * per : (s + 1) * per, :].astype(grads[s].dtype)


def down_kernel(rep, cap, rank, nb, *refs):
    vslot, tokens = refs[:2]
    parts = refs[2 : 2 + rep]
    down, a_all = refs[3 + rep : 5 + rep]
    turned = refs[5 + rep]
    per = cap * rank
    width = a_all.shape[1]
    for s in range(rep):
        a_all[s * per : (s + 1) * per, :] = parts[s][:, :width]
    chunk = 4
    for r in range(nb // chunk):
        prod = lax.dot_general(
            tokens[r * chunk * BLOCK : (r + 1) * chunk * BLOCK, :], a_all[...], NT, preferred_element_type=F32
        )
        for b in range(chunk):
            turned[r * chunk + b] = prod[b * BLOCK : (b + 1) * BLOCK, :].T
    for b in range(nb):
        start = pl.multiple_of(vslot[b] * rank, rank)
        down[:, b * BLOCK : (b + 1) * BLOCK] = turned[b, pl.ds(start, rank), :]


def grad_b_kernel(rep, cap, rank, nb, *refs):
    vslot, down_here, down_there, upstream = refs[:4]
    grads = refs[5:-1]
    spread = refs[-1]
    per = cap * rank
    cols = grads[0].shape[1]
    at = pl.multiple_of(lax.axis_index("tp") * cols, cols)
    spread[...] = jnp.zeros_like(spread)
    total = (SCALE * (down_here[...] + down_there[...])).astype(BF16)
    for b in range(nb):
        start = pl.multiple_of(vslot[b] * rank, rank)
        spread[pl.ds(start, rank), b * BLOCK : (b + 1) * BLOCK] = total[:, b * BLOCK : (b + 1) * BLOCK]
    grad = jnp.dot(spread[...], upstream[:, pl.ds(at, cols)], preferred_element_type=F32)
    for s in range(rep):
        grads[s][...] = grad[s * per : (s + 1) * per, :].astype(grads[s].dtype)


def token_kernel(chunk, tile, *refs):
    frozen, up_scaled, a_all = refs[:3]
    out, buf, sems = refs[-3:]
    rows, width = frozen.shape
    pending = {}
    for t in range(width // tile):
        slot = t % 2
        cols = slice(t * tile, (t + 1) * tile)
        for r in range(rows // chunk):
            at = slice(r * chunk, (r + 1) * chunk)
            if (slot, r) in pending:
                pending.pop((slot, r)).wait()
            low = jnp.dot(up_scaled[at, :], a_all[:, cols], preferred_element_type=F32)
            buf[slot, at, :] = (frozen[at, cols] + low).astype(BF16)
            copy = pltpu.make_async_copy(
                buf.at[slot, pl.ds(r * chunk, chunk), :],
                out.at[pl.ds(r * chunk, chunk), pl.ds(t * tile, tile)],
                sems.at[slot, r],
            )
            copy.start()
            pending[slot, r] = copy
    wait_all(pending.values())


def finish_kernel(rep, cap, rank, *refs):
    pick = refs[0]
    in_a = refs[1 : 1 + rep]
    in_b = refs[1 + rep : 1 + 2 * rep]
    out_a, out_b, sum_a, sum_b, sem = refs[2 + 2 * rep :]
    sum_a[...] = jnp.zeros_like(sum_a)
    sum_b[...] = jnp.zeros_like(sum_b)
    for s in range(rep):
        for c in range(cap):
            to = pick[s * cap + c]

            @pl.when(to >= 0)
            def _():
                sum_a[to] += in_a[s][c * rank : (c + 1) * rank, :].astype(F32)
                sum_b[to] += in_b[s][c * rank : (c + 1) * rank, :].astype(F32)

    wait_all(
        start_all(
            [pltpu.make_async_copy(sum_a, out_a, sem.at[0]), pltpu.make_async_copy(sum_b, out_b, sem.at[1])]
        )
    )


def local(tokens_in, upstream, base_weight, bank_a, bank_b, slot_ids, used_lists):
    rows, width = tokens_in.shape
    outs = upstream.shape[1]
    held, rank, cols = bank_b.shape
    slots = used_lists.shape[1]
    nb = rows // BLOCK
    rep = lax.axis_size("rep")
    tp = lax.axis_size("tp")
    cap = (slots + rep - 1) // rep
    per = cap * rank
    depth = rep * per
    tile = chunk = 512
    tie = lax.optimization_barrier

    def swap(axis, x, s):
        return lax.ppermute(x, axis, [(i, i ^ s) for i in range(lax.axis_size(axis))])

    def bits(n):
        return [1 << i for i in range(n.bit_length() - 1)]

    a_flat = in_hbm(bank_a.reshape(held * rank, width))
    b_flat = in_hbm(bank_b.reshape(held * rank, cols))
    vslot, bank = kernel(
        functools.partial(plan_kernel, cap, held),
        "plan",
        [struct((nb,), I32), pltpu.VMEM((held * rank, width + cols), BF16)],
        [HBM, HBM, HBM, HBM],
        [SMEM, VMEM],
        [in_hbm(used_lists), in_hbm(slot_ids.reshape(nb, BLOCK)), a_flat, b_flat],
        [
            pltpu.SMEM((1, slots), I32),
            pltpu.SMEM((nb, BLOCK), I32),
            pltpu.SMEM((slots,), I32),
            pltpu.SemaphoreType.DMA((4,)),
        ],
    )

    lists = tie((*[swap("rep", used_lists, s) for s in range(1, rep)], vslot, bank))
    *sends, pick = kernel(
        functools.partial(pick_kernel, rep, cap, held),
        "pick",
        [struct((per, width + cols), BF16)] * rep + [struct((rep * cap,), I32)],
        [ANY] * rep + [VMEM],
        [VMEM] * rep + [SMEM],
        [used_lists, *lists[: rep - 1], lists[rep]],
        [pltpu.SMEM((1, slots), I32)] * rep + [pltpu.SemaphoreType.DMA((rep,))],
    )
    vslot = lists[rep - 1]
    fetched = {s: swap("rep", sends[s], s) for s in range(rep - 1, 0, -1)}
    fetched[0] = sends[0]

    n_fetch = width // tile + 2 * (rows // chunk)
    frozen, upstream_v, tokens_v = kernel(
        functools.partial(frozen_kernel, chunk, tile),
        "frozen",
        [pltpu.VMEM((rows, width), F32), pltpu.VMEM((rows, outs), BF16), pltpu.VMEM((rows, width), BF16)],
        [HBM, HBM, HBM, ANY],
        [VMEM, VMEM, VMEM],
        [in_hbm(upstream), in_hbm(base_weight), in_hbm(tokens_in), sends[0]],
        [pltpu.VMEM((width, outs), BF16), pltpu.SemaphoreType.DMA((n_fetch,))],
    )
    *fetched, upstream_v, tokens_v, frozen = tie(
        (*[fetched[s] for s in range(rep)], upstream_v, tokens_v, frozen)
    )

    quarter = jnp.concatenate([x[:, width:] for x in fetched], axis=0)
    down, a_all = kernel(
        functools.partial(down_kernel, rep, cap, rank, nb),
        "down",
        [struct((rank, rows), F32), struct((depth, width), BF16)],
        [SMEM, VMEM] + [VMEM] * rep + [ANY],
        [VMEM, VMEM],
        [vslot, tokens_v, *fetched, quarter],
        [pltpu.VMEM((nb, depth, BLOCK), F32)],
    )
    held_q, came_q, order = quarter, None, [0]
    for bit in bits(tp)[::-1]:
        if came_q is not None:
            held_q = jnp.concatenate([held_q, came_q], axis=0)
            order += [s ^ (2 * bit) for s in order]
        came_q = swap("tp", held_q, bit)
        if bit == tp // 2:
            came_q, down = tie((came_q, down))
    for bit in bits(tp)[:-1]:
        down = down + swap("tp", down, bit)
    down_there = swap("tp", down, tp // 2)

    up_scaled, *grads_a = kernel(
        functools.partial(up_kernel, rep, cap, rank, nb, order),
        "up_grad_a",
        [struct((rows, depth), BF16), struct((per, width), F32)] + [struct((per, width), BF16)] * (rep - 1),
        [SMEM] + [VMEM] * 4 + [ANY],
        [VMEM] * (rep + 1),
        [vslot, upstream_v, held_q, came_q, tokens_v, down],
    )
    recv_ga = {s: swap("rep", grads_a[s], s) for s in range(rep - 1, 0, -1)}
    recv_ga[0] = grads_a[0]

    grads_b = kernel(
        functools.partial(grad_b_kernel, rep, cap, rank, nb),
        "grad_b",
        [struct((per, cols), F32)] + [struct((per, cols), BF16)] * (rep - 1),
        [SMEM, VMEM, VMEM, VMEM, ANY],
        [VMEM] * rep,
        [vslot, down, down_there, upstream_v, up_scaled],
        [pltpu.VMEM((depth, rows), BF16)],
    )
    recv_gb = {s: swap("rep", grads_b[s], s) for s in range(rep - 1, 0, -1)}
    recv_gb[0] = grads_b[0]

    token_gradient = kernel(
        functools.partial(token_kernel, chunk, tile),
        "token_gradient",
        pltpu.HBM((rows, width), BF16),
        [VMEM] * 3 + [ANY],
        HBM,
        [frozen, up_scaled, a_all, grads_b[0]],
        [pltpu.VMEM((2, rows, tile), BF16), pltpu.SemaphoreType.DMA((2, rows // chunk))],
    )

    grad_a, grad_b = kernel(
        functools.partial(finish_kernel, rep, cap, rank),
        "finish",
        [pltpu.HBM((held, rank, width), F32), pltpu.HBM((held, rank, cols), F32)],
        [SMEM] + [VMEM] * (2 * rep) + [HBM],
        [HBM] * 2,
        [pick, *[recv_ga[s] for s in range(rep)], *[recv_gb[s] for s in range(rep)], in_hbm(token_gradient)],
        [
            pltpu.VMEM((held, rank, width), F32),
            pltpu.VMEM((held, rank, cols), F32),
            pltpu.SemaphoreType.DMA((2,)),
        ],
    )
    return token_gradient, grad_a, grad_b


def solution(mesh):
    in_specs = (
        P(("groups", "rep"), "tp"),
        P(("groups", "rep"), None),
        P("tp", None),
        P("rep", None, "tp"),
        P("rep", None, "tp"),
        P(("groups", "rep")),
        P(("groups", "rep"), None),
    )
    out_specs = (
        P(("groups", "rep"), "tp"),
        P(("groups", "rep"), None, "tp"),
        P(("groups", "rep"), None, "tp"),
    )
    return jax.shard_map(local, mesh=mesh, in_specs=in_specs, out_specs=out_specs, check_vma=False)
```

```python
import functools

import jax
import jax.numpy as jnp
from jax import lax
from jax.experimental import pallas as pl
from jax.experimental.pallas import tpu as pltpu
from jax.sharding import PartitionSpec as P

BLOCK = 128
SCALE = 2.0
VMEM_LIMIT = 12 * 1024 * 1024

F32 = jnp.float32
BF16 = jnp.bfloat16
I32 = jnp.int32
ANY = pl.BlockSpec(memory_space=pl.ANY)
HBM = pl.BlockSpec(memory_space=pltpu.HBM)
SMEM = pl.BlockSpec(memory_space=pltpu.SMEM)
VMEM = pl.BlockSpec(memory_space=pltpu.VMEM)
NT = (((1,), (1,)), ((), ()))
TN = (((0,), (0,)), ((), ()))
struct = jax.ShapeDtypeStruct


def in_hbm(x):
    return pltpu.with_memory_space_constraint(x, pltpu.HBM)


def kernel(body, name, outs, in_specs, out_specs, args, scratch=(), alias=None, flops=0):
    return pl.pallas_call(
        body,
        out_shape=outs,
        in_specs=in_specs,
        out_specs=out_specs,
        scratch_shapes=list(scratch),
        input_output_aliases=alias or {},
        compiler_params=pltpu.CompilerParams(vmem_limit_bytes=VMEM_LIMIT),
        cost_estimate=pl.CostEstimate(flops=flops, bytes_accessed=0, transcendentals=0),
        name=name,
    )(*args)


def start_all(copies):
    for copy in copies:
        copy.start()
    return copies


def wait_all(copies):
    for copy in copies:
        copy.wait()


def split(ident, held):
    if held & (held - 1) == 0:
        shift = held.bit_length() - 1
        return lax.shift_right_logical(ident, I32(shift)), jnp.bitwise_and(ident, I32(held - 1))
    return lax.div(ident, I32(held)), lax.rem(ident, I32(held))


def plan_kernel(cap, held, *refs):
    my_list, slot_ids, bank_a, bank_b, upstream, weight = refs[:6]
    vslot, bank, upstream_v, weight_v = refs[6:10]
    lists, ids, place_v, sems = refs[10:]
    slots = lists.shape[1]
    width = bank_a.shape[1]
    half = upstream.shape[0] // 2
    copies = start_all(
        [
            pltpu.make_async_copy(my_list, lists, sems.at[0]),
            pltpu.make_async_copy(slot_ids, ids, sems.at[1]),
            pltpu.make_async_copy(bank_a, bank.at[:, pl.ds(0, width)], sems.at[2]),
            pltpu.make_async_copy(bank_b, bank.at[:, pl.ds(width, bank_b.shape[1])], sems.at[3]),
            pltpu.make_async_copy(weight.at[pl.ds(0, weight_v.shape[0]), :], weight_v, sems.at[4]),
            pltpu.make_async_copy(upstream.at[pl.ds(0, half), :], upstream_v.at[pl.ds(0, half), :], sems.at[5]),
        ]
    )
    me = lax.axis_index("rep")
    copies[0].wait()
    owners = [split(lists[0, k], held)[0] for k in range(slots)]
    for k in range(slots):
        place = I32(0)
        for j in range(k):
            place = place + (owners[j] == owners[k]).astype(I32)
        place_v[k] = jnp.bitwise_xor(owners[k], me) * cap + place
    copies[1].wait()
    for b in range(vslot.shape[0]):
        vslot[b] = place_v[ids[b, 0]]
    wait_all(copies[2:])


def pick_kernel(rep, cap, held, *refs):
    sources = refs[:rep]
    bank = refs[rep]
    outs = refs[rep + 1 : 2 * rep + 1]
    pick = refs[2 * rep + 1]
    lists = refs[2 * rep + 2 : 3 * rep + 2]
    sems = refs[3 * rep + 2]
    rank = outs[0].shape[0] // cap
    slots = lists[0].shape[1]
    me = lax.axis_index("rep")
    loads = start_all([pltpu.make_async_copy(sources[s], lists[s], sems.at[s]) for s in range(rep)])
    wait_all(loads)
    for s in range(rep):
        count = I32(0)
        idx = [I32(-1)] * cap
        for k in range(slots):
            owner, number = split(lists[s][0, k], held)
            mine = owner == me
            for c in range(cap):
                idx[c] = jnp.where(mine & (count == c), number, idx[c])
            count = count + mine.astype(I32)
        for c in range(cap):
            pick[s * cap + c] = idx[c]
            start = pl.multiple_of(jnp.maximum(idx[c], 0) * rank, rank)
            outs[s][c * rank : (c + 1) * rank, :] = bank[pl.ds(start, rank), :]


def frozen_kernel(chunk, tile, *refs):
    weight_first, weight, tokens, upstream_in_hbm = refs[1:5]
    out, tokens_v, upstream, weight_v, sems = refs[6:]
    rows = upstream.shape[0]

    def fetch(source, to, start, size, sem, base=0):
        return pltpu.make_async_copy(
            source.at[pl.ds(start, size), :], to.at[pl.ds(start - base, size), :], sems.at[sem]
        )

    half = rows // 2
    late = fetch(upstream_in_hbm, upstream, half, rows - half, sems.shape[0] - 1)
    late.start()
    starts = range(tile, weight.shape[0], tile)
    weights = start_all([fetch(weight, weight_v, at, tile, i, tile) for i, at in enumerate(starts)])
    toks = start_all([fetch(tokens, tokens_v, at, chunk, len(starts) + i) for i, at in enumerate(range(0, rows, chunk))])
    for t in range(len(starts) + 1):
        if t > 0:
            weights[t - 1].wait()
        cols = slice(t * tile, (t + 1) * tile)
        source = weight_first[...] if t == 0 else weight_v[(t - 1) * tile : t * tile, :]
        for r in range(rows // chunk):
            if t == 0 and r == half // chunk:
                late.wait()
            at = slice(r * chunk, (r + 1) * chunk)
            out[at, cols] = lax.dot_general(upstream[at, :], source, NT, preferred_element_type=F32)
    wait_all(toks)


def up_kernel(rep, cap, rank, nb, order, *refs):
    vslot, upstream, held_q, came_q, tokens = refs[:5]
    up_out = refs[6]
    grads, b_all = refs[7:-1], refs[-1]
    width = rep * cap * rank
    per = cap * rank
    cols = held_q.shape[1]
    tp_rank = lax.axis_index("tp")
    for i, s in enumerate(order):
        for j, piece in ((0, held_q), (1, came_q)):
            at = pl.multiple_of(jnp.bitwise_xor(tp_rank, s ^ j) * cols, cols)
            b_all[:, pl.ds(at, cols)] = piece[i * width : (i + 1) * width, :]
    chunk = 4
    lane_slot = lax.broadcasted_iota(I32, (BLOCK, width), 1) // rank
    for r in range(nb // chunk):
        rows = slice(r * chunk * BLOCK, (r + 1) * chunk * BLOCK)
        acc = lax.dot_general(upstream[rows, :], b_all[...], NT, preferred_element_type=F32)
        acc = (SCALE * acc).astype(BF16)
        for b in range(chunk):
            blk = r * chunk + b
            part = acc[b * BLOCK : (b + 1) * BLOCK, :]
            up_out[blk * BLOCK : (blk + 1) * BLOCK, :] = jnp.where(
                lane_slot == vslot[blk], part, jnp.zeros_like(part)
            )
    tile = 512
    for t in range(tokens.shape[1] // tile):
        at = slice(t * tile, (t + 1) * tile)
        grad = lax.dot_general(up_out[...], tokens[:, at], TN, preferred_element_type=F32)
        for s in range(rep):
            grads[s][:, at] = grad[s * per : (s + 1) * per, :].astype(grads[s].dtype)


def down_kernel(rep, cap, rank, nb, *refs):
    vslot, tokens = refs[:2]
    parts = refs[2 : 2 + rep]
    down, a_all = refs[3 + rep : 5 + rep]
    turned = refs[5 + rep]
    per = cap * rank
    width = a_all.shape[1]
    for s in range(rep):
        a_all[s * per : (s + 1) * per, :] = parts[s][:, :width]
    chunk = 4
    for r in range(nb // chunk):
        prod = lax.dot_general(
            tokens[r * chunk * BLOCK : (r + 1) * chunk * BLOCK, :], a_all[...], NT, preferred_element_type=F32
        )
        for b in range(chunk):
            turned[r * chunk + b] = prod[b * BLOCK : (b + 1) * BLOCK, :].T
    for b in range(nb):
        start = pl.multiple_of(vslot[b] * rank, rank)
        down[:, b * BLOCK : (b + 1) * BLOCK] = turned[b, pl.ds(start, rank), :]


def grad_b_kernel(rep, cap, rank, nb, *refs):
    vslot, down_here, down_there, upstream, near_a = refs[:5]
    grads = refs[5:-1]
    spread = refs[-1]
    per = cap * rank
    cols = grads[0].shape[1]
    at = pl.multiple_of(lax.axis_index("tp") * cols, cols)
    spread[...] = jnp.zeros_like(spread)
    total = (SCALE * (down_here[...] + down_there[...])).astype(BF16)
    for b in range(nb):
        start = pl.multiple_of(vslot[b] * rank, rank)
        spread[pl.ds(start, rank), b * BLOCK : (b + 1) * BLOCK] = total[:, b * BLOCK : (b + 1) * BLOCK]
    grad = jnp.dot(spread[...], upstream[:, pl.ds(at, cols)], preferred_element_type=F32)
    for s in range(rep):
        part = grad[s * per : (s + 1) * per, :].astype(grads[s].dtype)
        if s == 1:
            grads[s][:, : near_a.shape[1]] = near_a[...]
            grads[s][:, near_a.shape[1] :] = part
        else:
            grads[s][...] = part


def token_kernel(chunk, tiles, *refs):
    frozen, up_scaled, a_all = refs[:3]
    out, buf, sems = refs[-3:]
    rows = up_scaled.shape[0]
    pending = {}
    for n, (start, size) in enumerate(tiles):
        slot = n % 2
        cols = slice(start, start + size)
        for r in range(rows // chunk):
            at = slice(r * chunk, (r + 1) * chunk)
            if (slot, r) in pending:
                pending.pop((slot, r)).wait()
            total = jnp.dot(up_scaled[at, :], a_all[:, cols], preferred_element_type=F32)
            total = frozen[at, cols] + total
            buf[slot, at, :size] = total.astype(BF16)
            copy = pltpu.make_async_copy(
                buf.at[slot, pl.ds(r * chunk, chunk), pl.ds(0, size)],
                out.at[pl.ds(r * chunk, chunk), pl.ds(start, size)],
                sems.at[slot, r],
            )
            copy.start()
            pending[slot, r] = copy
    wait_all(pending.values())


def finish_kernel(rep, cap, rank, *refs):
    pick = refs[0]
    far = rep - 2
    near = refs[1 + far]
    own_a, own_b = refs[2 + 2 * far : 4 + 2 * far]
    in_a = (own_a, near, *refs[1 : 1 + far])
    in_b = (own_b, near, *refs[2 + far : 2 + 2 * far])
    out_a, out_b, sum_a, sum_b, sem = refs[1 + 2 * rep :]
    halves = 2
    width = sum_a.shape[2] // halves
    copies = []
    for h in range(halves):
        cols = slice(h * width, (h + 1) * width)
        sum_a[:, :, cols] = jnp.zeros(sum_a.shape[:2] + (width,), F32)
        if h == 0:
            sum_b[...] = jnp.zeros_like(sum_b)
        for s in range(rep):
            for c in range(cap):
                to = pick[s * cap + c]
                at = slice(c * rank, (c + 1) * rank)

                @pl.when(to >= 0)
                def _():
                    sum_a[to, :, cols] += in_a[s][at, cols].astype(F32)
                    if h == 0:
                        sum_b[to] += in_b[s][at, in_b[s].shape[1] - sum_b.shape[2] :].astype(F32)

        part = pl.ds(h * width, width)
        copies.append(pltpu.make_async_copy(sum_a.at[:, :, part], out_a.at[:, :, part], sem.at[h]))
        copies[-1].start()
        if h == 0:
            copies.append(pltpu.make_async_copy(sum_b, out_b, sem.at[halves]))
            copies[-1].start()
    wait_all(copies)


def local(tokens_in, upstream, base_weight, bank_a, bank_b, slot_ids, used_lists):
    rows, width = tokens_in.shape
    outs = upstream.shape[1]
    held, rank, cols = bank_b.shape
    slots = used_lists.shape[1]
    nb = rows // BLOCK
    rep = lax.axis_size("rep")
    tp = lax.axis_size("tp")
    cap = (slots + rep - 1) // rep
    per = cap * rank
    depth = rep * per
    tile = chunk = 512
    tie = lax.optimization_barrier

    def swap(axis, x, s):
        return lax.ppermute(x, axis, [(i, i ^ s) for i in range(lax.axis_size(axis))])

    def bits(n):
        return [1 << i for i in range(n.bit_length() - 1)]

    a_flat = in_hbm(bank_a.reshape(held * rank, width))
    b_flat = in_hbm(bank_b.reshape(held * rank, cols))
    w_flat = in_hbm(base_weight)
    vslot, bank, upstream_v, weight_first = kernel(
        functools.partial(plan_kernel, cap, held),
        "plan",
        [
            struct((nb,), I32),
            pltpu.VMEM((held * rank, width + cols), BF16),
            pltpu.VMEM((rows, outs), BF16),
            pltpu.VMEM((tile, outs), BF16),
        ],
        [HBM] * 6,
        [SMEM, VMEM, VMEM, VMEM],
        [
            in_hbm(used_lists),
            in_hbm(slot_ids.reshape(nb, BLOCK)),
            a_flat,
            b_flat,
            in_hbm(upstream),
            w_flat,
        ],
        [
            pltpu.SMEM((1, slots), I32),
            pltpu.SMEM((nb, BLOCK), I32),
            pltpu.SMEM((slots,), I32),
            pltpu.SemaphoreType.DMA((6,)),
        ],
    )

    lists = tie((*[swap("rep", used_lists, s) for s in range(1, rep)], vslot, bank))
    *sends, pick = kernel(
        functools.partial(pick_kernel, rep, cap, held),
        "pick",
        [struct((per, width + cols), BF16)] * rep + [struct((rep * cap,), I32)],
        [HBM] + [ANY] * (rep - 1) + [VMEM],
        [VMEM] * rep + [SMEM],
        [in_hbm(used_lists), *lists[: rep - 1], lists[rep]],
        [pltpu.SMEM((1, slots), I32)] * rep + [pltpu.SemaphoreType.DMA((rep,))],
    )
    vslot = lists[rep - 1]
    fetched = {s: swap("rep", sends[s], s) for s in range(1, rep)}
    fetched[0] = sends[0]

    frozen, tokens_v, upstream_v = kernel(
        functools.partial(frozen_kernel, chunk, tile),
        "frozen",
        [pltpu.VMEM((rows, width), F32), pltpu.VMEM((rows, width), BF16), pltpu.VMEM((rows, outs), BF16)],
        [VMEM, VMEM, HBM, HBM, HBM, ANY],
        [VMEM] * 3,
        [upstream_v, weight_first, w_flat, in_hbm(tokens_in), in_hbm(upstream), sends[0]],
        [
            pltpu.VMEM((width - tile, outs), BF16),
            pltpu.SemaphoreType.DMA((width // tile + rows // chunk,)),
        ],
        {0: 2},
    )
    *far, upstream_v, tokens_v, frozen = tie((*[fetched[s] for s in range(2, rep)], upstream_v, tokens_v, frozen))
    *fetched, upstream_v = tie((fetched[0], fetched[1], *far, upstream_v))

    quarter = jnp.concatenate([x[:, width:] for x in fetched], axis=0)
    down, a_all = kernel(
        functools.partial(down_kernel, rep, cap, rank, nb),
        "down",
        [struct((rank, rows), F32), struct((depth, width), BF16)],
        [SMEM, VMEM] + [VMEM] * rep + [ANY],
        [VMEM, VMEM],
        [vslot, tokens_v, *fetched, quarter],
        [pltpu.VMEM((nb, depth, BLOCK), F32)],
    )
    held_q, came_q, order = quarter, None, [0]
    for bit in bits(tp)[::-1]:
        if came_q is not None:
            held_q = jnp.concatenate([held_q, came_q], axis=0)
            order += [s ^ (2 * bit) for s in order]
        came_q = swap("tp", held_q, bit)
        if bit == tp // 2:
            came_q, down = tie((came_q, down))
    for bit in bits(tp)[:-1]:
        down = down + swap("tp", down, bit)
    down_there = swap("tp", down, tp // 2)

    up_scaled, *grads_a = kernel(
        functools.partial(up_kernel, rep, cap, rank, nb, order),
        "up_grad_a",
        [struct((rows, depth), BF16), struct((per, width), F32)] + [struct((per, width), BF16)] * (rep - 1),
        [SMEM] + [VMEM] * 4 + [ANY],
        [VMEM] * (rep + 1),
        [vslot, upstream_v, held_q, came_q, tokens_v, down],
        [pltpu.VMEM((depth, outs), BF16)],
    )
    grads_b = kernel(
        functools.partial(grad_b_kernel, rep, cap, rank, nb),
        "grad_b",
        [struct((per, cols), F32), struct((per, width + cols), BF16)] + [struct((per, cols), BF16)] * (rep - 2),
        [SMEM] + [VMEM] * 4,
        [VMEM] * rep,
        [vslot, down, down_there, upstream_v, grads_a[1]],
        [pltpu.VMEM((depth, rows), BF16)],
    )
    far_a = [swap("rep", grads_a[s], s) for s in range(2, rep)]
    near = swap("rep", grads_b[1], 1)
    far_b = [swap("rep", grads_b[s], s) for s in range(2, rep)]

    token_gradient = kernel(
        functools.partial(token_kernel, chunk, [(at, tile) for at in range(0, width, tile)]),
        "token_gradient",
        pltpu.HBM((rows, width), BF16),
        [VMEM] * 3 + [ANY],
        HBM,
        [frozen, up_scaled, a_all, grads_b[0]],
        [pltpu.VMEM((2, rows, tile), BF16), pltpu.SemaphoreType.DMA((2, rows // chunk))],
        flops=8 * rows * width * depth,
    )

    grad_a, grad_b = kernel(
        functools.partial(finish_kernel, rep, cap, rank),
        "finish",
        [pltpu.HBM((held, rank, width), F32), pltpu.HBM((held, rank, cols), F32)],
        [SMEM] + [VMEM] * (2 * rep - 1) + [HBM],
        [HBM] * 2,
        [pick, *far_a, near, *far_b, grads_a[0], grads_b[0], in_hbm(token_gradient)],
        [
            pltpu.VMEM((held, rank, width), F32),
            pltpu.VMEM((held, rank, cols), F32),
            pltpu.SemaphoreType.DMA((3,)),
        ],
    )
    return token_gradient, grad_a, grad_b


def solution(mesh):
    in_specs = (
        P(("groups", "rep"), "tp"),
        P(("groups", "rep"), None),
        P("tp", None),
        P("rep", None, "tp"),
        P("rep", None, "tp"),
        P(("groups", "rep")),
        P(("groups", "rep"), None),
    )
    out_specs = (
        P(("groups", "rep"), "tp"),
        P(("groups", "rep"), None, "tp"),
        P(("groups", "rep"), None, "tp"),
    )
    return jax.shard_map(local, mesh=mesh, in_specs=in_specs, out_specs=out_specs, check_vma=False)
```

```python
import functools

import jax
import jax.numpy as jnp
from jax import lax
from jax.experimental import pallas as pl
from jax.experimental.pallas import tpu as pltpu
from jax.sharding import PartitionSpec as P

BLOCK = 128
SCALE = 2.0
VMEM_LIMIT = 12 * 1024 * 1024

F32 = jnp.float32
BF16 = jnp.bfloat16
I32 = jnp.int32
ANY = pl.BlockSpec(memory_space=pl.ANY)
HBM = pl.BlockSpec(memory_space=pltpu.HBM)
SMEM = pl.BlockSpec(memory_space=pltpu.SMEM)
VMEM = pl.BlockSpec(memory_space=pltpu.VMEM)
NT = (((1,), (1,)), ((), ()))
TN = (((0,), (0,)), ((), ()))
struct = jax.ShapeDtypeStruct


def in_hbm(x):
    return pltpu.with_memory_space_constraint(x, pltpu.HBM)


def kernel(body, name, outs, in_specs, out_specs, args, scratch=(), alias=None, flops=0):
    return pl.pallas_call(
        body,
        out_shape=outs,
        in_specs=in_specs,
        out_specs=out_specs,
        scratch_shapes=list(scratch),
        input_output_aliases=alias or {},
        compiler_params=pltpu.CompilerParams(vmem_limit_bytes=VMEM_LIMIT),
        cost_estimate=pl.CostEstimate(flops=flops, bytes_accessed=0, transcendentals=0),
        name=name,
    )(*args)


def start_all(copies):
    for copy in copies:
        copy.start()
    return copies


def wait_all(copies):
    for copy in copies:
        copy.wait()


def split(ident, held):
    if held & (held - 1) == 0:
        shift = held.bit_length() - 1
        return lax.shift_right_logical(ident, I32(shift)), jnp.bitwise_and(ident, I32(held - 1))
    return lax.div(ident, I32(held)), lax.rem(ident, I32(held))


def plan_kernel(cap, held, *refs):
    my_list, slot_ids, bank_a, bank_b, upstream, weight = refs[:6]
    vslot, bank, upstream_v, weight_v = refs[6:10]
    lists, ids, place_v, sems = refs[10:]
    slots = lists.shape[1]
    width = bank_a.shape[1]
    half = upstream.shape[0] // 2
    copies = start_all(
        [
            pltpu.make_async_copy(my_list, lists, sems.at[0]),
            pltpu.make_async_copy(slot_ids, ids, sems.at[1]),
            pltpu.make_async_copy(bank_a, bank.at[:, pl.ds(0, width)], sems.at[2]),
            pltpu.make_async_copy(bank_b, bank.at[:, pl.ds(width, bank_b.shape[1])], sems.at[3]),
            pltpu.make_async_copy(weight.at[pl.ds(0, weight_v.shape[0]), :], weight_v, sems.at[4]),
            pltpu.make_async_copy(upstream.at[pl.ds(0, half), :], upstream_v.at[pl.ds(0, half), :], sems.at[5]),
        ]
    )
    me = lax.axis_index("rep")
    copies[0].wait()
    owners = [split(lists[0, k], held)[0] for k in range(slots)]
    for k in range(slots):
        place = I32(0)
        for j in range(k):
            place = place + (owners[j] == owners[k]).astype(I32)
        place_v[k] = jnp.bitwise_xor(owners[k], me) * cap + place
    copies[1].wait()
    for b in range(vslot.shape[0]):
        vslot[b] = place_v[ids[b, 0]]
    wait_all(copies[2:])


def pick_kernel(rep, cap, held, *refs):
    sources = refs[:rep]
    bank = refs[rep]
    outs = refs[rep + 1 : 2 * rep + 1]
    pick = refs[2 * rep + 1]
    lists = refs[2 * rep + 2 : 3 * rep + 2]
    sems = refs[3 * rep + 2]
    rank = outs[0].shape[0] // cap
    slots = lists[0].shape[1]
    me = lax.axis_index("rep")
    loads = start_all([pltpu.make_async_copy(sources[s], lists[s], sems.at[s]) for s in range(rep)])
    wait_all(loads)
    for s in range(rep):
        count = I32(0)
        idx = [I32(-1)] * cap
        for k in range(slots):
            owner, number = split(lists[s][0, k], held)
            mine = owner == me
            for c in range(cap):
                idx[c] = jnp.where(mine & (count == c), number, idx[c])
            count = count + mine.astype(I32)
        for c in range(cap):
            pick[s * cap + c] = idx[c]
            start = pl.multiple_of(jnp.maximum(idx[c], 0) * rank, rank)
            outs[s][c * rank : (c + 1) * rank, :] = bank[pl.ds(start, rank), :]


def frozen_kernel(chunk, tile, *refs):
    weight_first, weight, tokens, upstream_in_hbm = refs[1:5]
    out, tokens_v, upstream, weight_v, sems = refs[6:]
    rows = upstream.shape[0]

    def fetch(source, to, start, size, sem, base=0):
        return pltpu.make_async_copy(
            source.at[pl.ds(start, size), :], to.at[pl.ds(start - base, size), :], sems.at[sem]
        )

    half = rows // 2
    late = fetch(upstream_in_hbm, upstream, half, rows - half, sems.shape[0] - 1)
    late.start()
    starts = range(tile, weight.shape[0], tile)
    weights = start_all([fetch(weight, weight_v, at, tile, i, tile) for i, at in enumerate(starts)])
    toks = start_all([fetch(tokens, tokens_v, at, chunk, len(starts) + i) for i, at in enumerate(range(0, rows, chunk))])
    for t in range(len(starts) + 1):
        if t > 0:
            weights[t - 1].wait()
        cols = slice(t * tile, (t + 1) * tile)
        source = weight_first[...] if t == 0 else weight_v[(t - 1) * tile : t * tile, :]
        for r in range(rows // chunk):
            if t == 0 and r == half // chunk:
                late.wait()
            at = slice(r * chunk, (r + 1) * chunk)
            out[at, cols] = lax.dot_general(upstream[at, :], source, NT, preferred_element_type=F32)
    wait_all(toks)


def up_terms(upstream, rows, piece, owners, width):
    cols = piece.shape[1]
    tp_rank = lax.axis_index("tp")
    acc = None
    for i, s in enumerate(owners):
        at = pl.multiple_of(jnp.bitwise_xor(tp_rank, s) * cols, cols)
        part = lax.dot_general(
            upstream[rows, pl.ds(at, cols)], piece[i * width : (i + 1) * width, :], NT, preferred_element_type=F32
        )
        acc = part if acc is None else acc + part
    return acc


def up_first_kernel(chunk, order, upstream, held_q, out):
    for r in range(out.shape[0] // chunk):
        rows = slice(r * chunk, (r + 1) * chunk)
        out[rows, :] = up_terms(upstream, rows, held_q, order, out.shape[1])


def up_kernel(rep, cap, rank, nb, order, *refs):
    vslot, upstream, up_first, came_q, tokens = refs[:5]
    up_out = refs[6]
    grads = refs[7:]
    width = rep * cap * rank
    per = cap * rank
    chunk = 4
    lane_slot = lax.broadcasted_iota(I32, (BLOCK, width), 1) // rank
    for r in range(nb // chunk):
        rows = slice(r * chunk * BLOCK, (r + 1) * chunk * BLOCK)
        acc = up_first[rows, :] + up_terms(upstream, rows, came_q, [s ^ 1 for s in order], width)
        acc = (SCALE * acc).astype(BF16)
        for b in range(chunk):
            blk = r * chunk + b
            part = acc[b * BLOCK : (b + 1) * BLOCK, :]
            up_out[blk * BLOCK : (blk + 1) * BLOCK, :] = jnp.where(
                lane_slot == vslot[blk], part, jnp.zeros_like(part)
            )
    tile = 512
    for t in range(tokens.shape[1] // tile):
        at = slice(t * tile, (t + 1) * tile)
        grad = lax.dot_general(up_out[...], tokens[:, at], TN, preferred_element_type=F32)
        for s in range(rep):
            grads[s][:, at] = grad[s * per : (s + 1) * per, :].astype(grads[s].dtype)


def down_kernel(rep, cap, rank, nb, *refs):
    vslot, tokens = refs[:2]
    parts = refs[2 : 2 + rep]
    down, a_all = refs[3 + rep : 5 + rep]
    turned = refs[5 + rep]
    per = cap * rank
    width = a_all.shape[1]
    for s in range(rep):
        a_all[s * per : (s + 1) * per, :] = parts[s][:, :width]
    chunk = 4
    for r in range(nb // chunk):
        prod = lax.dot_general(
            tokens[r * chunk * BLOCK : (r + 1) * chunk * BLOCK, :], a_all[...], NT, preferred_element_type=F32
        )
        for b in range(chunk):
            turned[r * chunk + b] = prod[b * BLOCK : (b + 1) * BLOCK, :].T
    for b in range(nb):
        start = pl.multiple_of(vslot[b] * rank, rank)
        down[:, b * BLOCK : (b + 1) * BLOCK] = turned[b, pl.ds(start, rank), :]


def grad_b_kernel(rep, cap, rank, nb, *refs):
    vslot, down_here, down_there, upstream, near_a = refs[:5]
    grads = refs[5:-1]
    spread = refs[-1]
    per = cap * rank
    cols = grads[0].shape[1]
    at = pl.multiple_of(lax.axis_index("tp") * cols, cols)
    spread[...] = jnp.zeros_like(spread)
    total = (SCALE * (down_here[...] + down_there[...])).astype(BF16)
    for b in range(nb):
        start = pl.multiple_of(vslot[b] * rank, rank)
        spread[pl.ds(start, rank), b * BLOCK : (b + 1) * BLOCK] = total[:, b * BLOCK : (b + 1) * BLOCK]
    grad = jnp.dot(spread[...], upstream[:, pl.ds(at, cols)], preferred_element_type=F32)
    for s in range(rep):
        part = grad[s * per : (s + 1) * per, :].astype(grads[s].dtype)
        if s == 1:
            grads[s][:, : near_a.shape[1]] = near_a[...]
            grads[s][:, near_a.shape[1] :] = part
        else:
            grads[s][...] = part


def token_kernel(chunk, tiles, *refs):
    frozen, up_scaled, a_all = refs[:3]
    out, buf, sems = refs[-3:]
    rows = up_scaled.shape[0]
    pending = {}
    for n, (start, size) in enumerate(tiles):
        slot = n % 2
        cols = slice(start, start + size)
        for r in range(rows // chunk):
            at = slice(r * chunk, (r + 1) * chunk)
            if (slot, r) in pending:
                pending.pop((slot, r)).wait()
            total = jnp.dot(up_scaled[at, :], a_all[:, cols], preferred_element_type=F32)
            total = frozen[at, cols] + total
            buf[slot, at, :size] = total.astype(BF16)
            copy = pltpu.make_async_copy(
                buf.at[slot, pl.ds(r * chunk, chunk), pl.ds(0, size)],
                out.at[pl.ds(r * chunk, chunk), pl.ds(start, size)],
                sems.at[slot, r],
            )
            copy.start()
            pending[slot, r] = copy
    wait_all(pending.values())


def finish_kernel(rep, cap, rank, *refs):
    pick = refs[0]
    far = rep - 2
    near = refs[1 + far]
    own_a, own_b = refs[2 + 2 * far : 4 + 2 * far]
    in_a = (own_a, near, *refs[1 : 1 + far])
    in_b = (own_b, near, *refs[2 + far : 2 + 2 * far])
    out_a, out_b, sum_a, sum_b, sem = refs[1 + 2 * rep :]
    halves = 2
    width = sum_a.shape[2] // halves
    copies = []
    for h in range(halves):
        cols = slice(h * width, (h + 1) * width)
        sum_a[:, :, cols] = jnp.zeros(sum_a.shape[:2] + (width,), F32)
        if h == 0:
            sum_b[...] = jnp.zeros_like(sum_b)
        for s in range(rep):
            for c in range(cap):
                to = pick[s * cap + c]
                at = slice(c * rank, (c + 1) * rank)

                @pl.when(to >= 0)
                def _():
                    sum_a[to, :, cols] += in_a[s][at, cols].astype(F32)
                    if h == 0:
                        sum_b[to] += in_b[s][at, in_b[s].shape[1] - sum_b.shape[2] :].astype(F32)

        part = pl.ds(h * width, width)
        copies.append(pltpu.make_async_copy(sum_a.at[:, :, part], out_a.at[:, :, part], sem.at[h]))
        copies[-1].start()
        if h == 0:
            copies.append(pltpu.make_async_copy(sum_b, out_b, sem.at[halves]))
            copies[-1].start()
    wait_all(copies)


def local(tokens_in, upstream, base_weight, bank_a, bank_b, slot_ids, used_lists):
    rows, width = tokens_in.shape
    outs = upstream.shape[1]
    held, rank, cols = bank_b.shape
    slots = used_lists.shape[1]
    nb = rows // BLOCK
    rep = lax.axis_size("rep")
    tp = lax.axis_size("tp")
    cap = (slots + rep - 1) // rep
    per = cap * rank
    depth = rep * per
    tile = chunk = 512
    tie = lax.optimization_barrier

    def swap(axis, x, s):
        return lax.ppermute(x, axis, [(i, i ^ s) for i in range(lax.axis_size(axis))])

    def bits(n):
        return [1 << i for i in range(n.bit_length() - 1)]

    a_flat = in_hbm(bank_a.reshape(held * rank, width))
    b_flat = in_hbm(bank_b.reshape(held * rank, cols))
    w_flat = in_hbm(base_weight)
    vslot, bank, upstream_v, weight_first = kernel(
        functools.partial(plan_kernel, cap, held),
        "plan",
        [
            struct((nb,), I32),
            pltpu.VMEM((held * rank, width + cols), BF16),
            pltpu.VMEM((rows, outs), BF16),
            pltpu.VMEM((tile, outs), BF16),
        ],
        [HBM] * 6,
        [SMEM, VMEM, VMEM, VMEM],
        [
            in_hbm(used_lists),
            in_hbm(slot_ids.reshape(nb, BLOCK)),
            a_flat,
            b_flat,
            in_hbm(upstream),
            w_flat,
        ],
        [
            pltpu.SMEM((1, slots), I32),
            pltpu.SMEM((nb, BLOCK), I32),
            pltpu.SMEM((slots,), I32),
            pltpu.SemaphoreType.DMA((6,)),
        ],
    )

    lists = tie((*[swap("rep", used_lists, s) for s in range(1, rep)], vslot, bank))
    *sends, pick = kernel(
        functools.partial(pick_kernel, rep, cap, held),
        "pick",
        [struct((per, width + cols), BF16)] * rep + [struct((rep * cap,), I32)],
        [HBM] + [ANY] * (rep - 1) + [VMEM],
        [VMEM] * rep + [SMEM],
        [in_hbm(used_lists), *lists[: rep - 1], lists[rep]],
        [pltpu.SMEM((1, slots), I32)] * rep + [pltpu.SemaphoreType.DMA((rep,))],
    )
    vslot = lists[rep - 1]
    fetched = {s: swap("rep", sends[s], s) for s in range(1, rep)}
    fetched[0] = sends[0]

    frozen, tokens_v, upstream_v = kernel(
        functools.partial(frozen_kernel, chunk, tile),
        "frozen",
        [pltpu.VMEM((rows, width), F32), pltpu.VMEM((rows, width), BF16), pltpu.VMEM((rows, outs), BF16)],
        [VMEM, VMEM, HBM, HBM, HBM, ANY],
        [VMEM] * 3,
        [upstream_v, weight_first, w_flat, in_hbm(tokens_in), in_hbm(upstream), sends[0]],
        [
            pltpu.VMEM((width - tile, outs), BF16),
            pltpu.SemaphoreType.DMA((width // tile + rows // chunk,)),
        ],
        {0: 2},
    )
    *far, upstream_v, tokens_v, frozen = tie((*[fetched[s] for s in range(2, rep)], upstream_v, tokens_v, frozen))
    *fetched, upstream_v = tie((fetched[0], fetched[1], *far, upstream_v))

    quarter = jnp.concatenate([x[:, width:] for x in fetched], axis=0)
    down, a_all = kernel(
        functools.partial(down_kernel, rep, cap, rank, nb),
        "down",
        [struct((rank, rows), F32), struct((depth, width), BF16)],
        [SMEM, VMEM] + [VMEM] * rep + [ANY],
        [VMEM, VMEM],
        [vslot, tokens_v, *fetched, quarter],
        [pltpu.VMEM((nb, depth, BLOCK), F32)],
    )
    held_q, came_q, order = quarter, None, [0]
    for bit in bits(tp)[::-1]:
        if came_q is not None:
            held_q = jnp.concatenate([held_q, came_q], axis=0)
            order += [s ^ (2 * bit) for s in order]
        came_q = swap("tp", held_q, bit)
        if bit == tp // 2:
            came_q, down = tie((came_q, down))
    up_first = kernel(
        functools.partial(up_first_kernel, chunk, order),
        "up_first",
        pltpu.VMEM((rows, depth), F32),
        [VMEM] * 2,
        VMEM,
        [upstream_v, held_q],
    )
    for bit in bits(tp)[:-1]:
        came = swap("tp", down, bit)
        if bit == 1:
            came, up_first = tie((came, up_first))
        down = down + came
    down_there = swap("tp", down, tp // 2)

    up_scaled, *grads_a = kernel(
        functools.partial(up_kernel, rep, cap, rank, nb, order),
        "up_grad_a",
        [struct((rows, depth), BF16), struct((per, width), F32)] + [struct((per, width), BF16)] * (rep - 1),
        [SMEM] + [VMEM] * 4 + [ANY],
        [VMEM] * (rep + 1),
        [vslot, upstream_v, up_first, came_q, tokens_v, down],
    )
    grads_b = kernel(
        functools.partial(grad_b_kernel, rep, cap, rank, nb),
        "grad_b",
        [struct((per, cols), F32), struct((per, width + cols), BF16)] + [struct((per, cols), BF16)] * (rep - 2),
        [SMEM] + [VMEM] * 4,
        [VMEM] * rep,
        [vslot, down, down_there, upstream_v, grads_a[1]],
        [pltpu.VMEM((depth, rows), BF16)],
    )
    far_a = [swap("rep", grads_a[s], s) for s in range(2, rep)]
    near = swap("rep", grads_b[1], 1)
    far_b = [swap("rep", grads_b[s], s) for s in range(2, rep)]

    token_gradient = kernel(
        functools.partial(token_kernel, chunk, [(at, tile) for at in range(0, width, tile)]),
        "token_gradient",
        pltpu.HBM((rows, width), BF16),
        [VMEM] * 3 + [ANY],
        HBM,
        [frozen, up_scaled, a_all, grads_b[0]],
        [pltpu.VMEM((2, rows, tile), BF16), pltpu.SemaphoreType.DMA((2, rows // chunk))],
        flops=8 * rows * width * depth,
    )

    grad_a, grad_b = kernel(
        functools.partial(finish_kernel, rep, cap, rank),
        "finish",
        [pltpu.HBM((held, rank, width), F32), pltpu.HBM((held, rank, cols), F32)],
        [SMEM] + [VMEM] * (2 * rep - 1) + [HBM],
        [HBM] * 2,
        [pick, *far_a, near, *far_b, grads_a[0], grads_b[0], in_hbm(token_gradient)],
        [
            pltpu.VMEM((held, rank, width), F32),
            pltpu.VMEM((held, rank, cols), F32),
            pltpu.SemaphoreType.DMA((3,)),
        ],
    )
    return token_gradient, grad_a, grad_b


def solution(mesh):
    in_specs = (
        P(("groups", "rep"), "tp"),
        P(("groups", "rep"), None),
        P("tp", None),
        P("rep", None, "tp"),
        P("rep", None, "tp"),
        P(("groups", "rep")),
        P(("groups", "rep"), None),
    )
    out_specs = (
        P(("groups", "rep"), "tp"),
        P(("groups", "rep"), None, "tp"),
        P(("groups", "rep"), None, "tp"),
    )
    return jax.shard_map(local, mesh=mesh, in_specs=in_specs, out_specs=out_specs, check_vma=False)
```

```python
import functools

import jax
import jax.numpy as jnp
from jax import lax
from jax.experimental import pallas as pl
from jax.experimental.pallas import tpu as pltpu
from jax.sharding import PartitionSpec as P

BLOCK = 128
SCALE = 2.0
VMEM_LIMIT = 12 * 1024 * 1024

F32 = jnp.float32
BF16 = jnp.bfloat16
I32 = jnp.int32
ANY = pl.BlockSpec(memory_space=pl.ANY)
HBM = pl.BlockSpec(memory_space=pltpu.HBM)
SMEM = pl.BlockSpec(memory_space=pltpu.SMEM)
VMEM = pl.BlockSpec(memory_space=pltpu.VMEM)
NT = (((1,), (1,)), ((), ()))
TN = (((0,), (0,)), ((), ()))
struct = jax.ShapeDtypeStruct


def in_hbm(x):
    return pltpu.with_memory_space_constraint(x, pltpu.HBM)


def kernel(body, name, outs, in_specs, out_specs, args, scratch=(), alias=None, flops=0):
    return pl.pallas_call(
        body,
        out_shape=outs,
        in_specs=in_specs,
        out_specs=out_specs,
        scratch_shapes=list(scratch),
        input_output_aliases=alias or {},
        compiler_params=pltpu.CompilerParams(vmem_limit_bytes=VMEM_LIMIT),
        cost_estimate=pl.CostEstimate(flops=flops, bytes_accessed=0, transcendentals=0),
        name=name,
    )(*args)


def start_all(copies):
    for copy in copies:
        copy.start()
    return copies


def wait_all(copies):
    for copy in copies:
        copy.wait()


def split(ident, held):
    if held & (held - 1) == 0:
        shift = held.bit_length() - 1
        return lax.shift_right_logical(ident, I32(shift)), jnp.bitwise_and(ident, I32(held - 1))
    return lax.div(ident, I32(held)), lax.rem(ident, I32(held))


def plan_kernel(cap, held, *refs):
    my_list, slot_ids, bank_a, bank_b, upstream, weight = refs[:6]
    vslot, bank, upstream_v, weight_v, my_list_v = refs[6:11]
    lists, ids, place_v, sems = refs[11:]
    slots = lists.shape[1]
    width = bank_a.shape[1]
    half = upstream.shape[0] // 2
    copies = start_all(
        [
            pltpu.make_async_copy(my_list, lists, sems.at[0]),
            pltpu.make_async_copy(slot_ids, ids, sems.at[1]),
            pltpu.make_async_copy(bank_a, bank.at[:, pl.ds(0, width)], sems.at[2]),
            pltpu.make_async_copy(bank_b, bank.at[:, pl.ds(width, bank_b.shape[1])], sems.at[3]),
            pltpu.make_async_copy(my_list, my_list_v, sems.at[6]),
            pltpu.make_async_copy(weight.at[pl.ds(0, weight_v.shape[0]), :], weight_v, sems.at[4]),
            pltpu.make_async_copy(upstream.at[pl.ds(0, half), :], upstream_v.at[pl.ds(0, half), :], sems.at[5]),
        ]
    )
    me = lax.axis_index("rep")
    copies[0].wait()
    owners = [split(lists[0, k], held)[0] for k in range(slots)]
    for k in range(slots):
        place = I32(0)
        for j in range(k):
            place = place + (owners[j] == owners[k]).astype(I32)
        place_v[k] = jnp.bitwise_xor(owners[k], me) * cap + place
    copies[1].wait()
    for b in range(vslot.shape[0]):
        vslot[b] = place_v[ids[b, 0]]
    wait_all(copies[2:])


def pick_kernel(rep, cap, held, *refs):
    sources = refs[:rep]
    bank = refs[rep]
    outs = refs[rep + 1 : 2 * rep + 1]
    pick = refs[2 * rep + 1]
    lists = refs[2 * rep + 2 : 3 * rep + 2]
    sems = refs[3 * rep + 2]
    rank = outs[0].shape[0] // cap
    slots = lists[0].shape[1]
    me = lax.axis_index("rep")
    loads = start_all([pltpu.make_async_copy(sources[s], lists[s], sems.at[s]) for s in range(rep)])
    wait_all(loads)
    for s in range(rep):
        count = I32(0)
        idx = [I32(-1)] * cap
        for k in range(slots):
            owner, number = split(lists[s][0, k], held)
            mine = owner == me
            for c in range(cap):
                idx[c] = jnp.where(mine & (count == c), number, idx[c])
            count = count + mine.astype(I32)
        for c in range(cap):
            pick[s * cap + c] = idx[c]
            start = pl.multiple_of(jnp.maximum(idx[c], 0) * rank, rank)
            outs[s][c * rank : (c + 1) * rank, :] = bank[pl.ds(start, rank), :]


def frozen_kernel(chunk, tile, *refs):
    weight_first, weight, tokens, upstream_in_hbm = refs[1:5]
    out, tokens_v, upstream, weight_v, sems = refs[6:]
    rows = upstream.shape[0]

    def fetch(source, to, start, size, sem, base=0):
        return pltpu.make_async_copy(
            source.at[pl.ds(start, size), :], to.at[pl.ds(start - base, size), :], sems.at[sem]
        )

    half = rows // 2
    late = fetch(upstream_in_hbm, upstream, half, rows - half, sems.shape[0] - 1)
    late.start()
    starts = range(tile, weight.shape[0], tile)
    weights = start_all([fetch(weight, weight_v, at, tile, i, tile) for i, at in enumerate(starts)])
    toks = start_all([fetch(tokens, tokens_v, at, chunk, len(starts) + i) for i, at in enumerate(range(0, rows, chunk))])
    for t in range(len(starts) + 1):
        if t > 0:
            weights[t - 1].wait()
        cols = slice(t * tile, (t + 1) * tile)
        source = weight_first[...] if t == 0 else weight_v[(t - 1) * tile : t * tile, :]
        for r in range(rows // chunk):
            if t == 0 and r == half // chunk:
                late.wait()
            at = slice(r * chunk, (r + 1) * chunk)
            out[at, cols] = lax.dot_general(upstream[at, :], source, NT, preferred_element_type=F32)
    wait_all(toks)


def up_terms(upstream, rows, piece, owners, width):
    cols = piece.shape[1]
    tp_rank = lax.axis_index("tp")
    acc = None
    for i, s in enumerate(owners):
        at = pl.multiple_of(jnp.bitwise_xor(tp_rank, s) * cols, cols)
        part = lax.dot_general(
            upstream[rows, pl.ds(at, cols)], piece[i * width : (i + 1) * width, :], NT, preferred_element_type=F32
        )
        acc = part if acc is None else acc + part
    return acc


def up_first_kernel(chunk, order, upstream, held_q, out):
    for r in range(out.shape[0] // chunk):
        rows = slice(r * chunk, (r + 1) * chunk)
        out[rows, :] = up_terms(upstream, rows, held_q, order, out.shape[1])


def up_kernel(rep, cap, rank, nb, order, *refs):
    vslot, upstream, up_first, came_q, tokens = refs[:5]
    up_out = refs[6]
    grads = refs[7:]
    width = rep * cap * rank
    per = cap * rank
    chunk = 4
    lane_slot = lax.broadcasted_iota(I32, (BLOCK, width), 1) // rank
    for r in range(nb // chunk):
        rows = slice(r * chunk * BLOCK, (r + 1) * chunk * BLOCK)
        acc = up_first[rows, :] + up_terms(upstream, rows, came_q, [s ^ 1 for s in order], width)
        acc = (SCALE * acc).astype(BF16)
        for b in range(chunk):
            blk = r * chunk + b
            part = acc[b * BLOCK : (b + 1) * BLOCK, :]
            up_out[blk * BLOCK : (blk + 1) * BLOCK, :] = jnp.where(
                lane_slot == vslot[blk], part, jnp.zeros_like(part)
            )
    tile = 512
    for t in range(tokens.shape[1] // tile):
        at = slice(t * tile, (t + 1) * tile)
        grad = lax.dot_general(up_out[...], tokens[:, at], TN, preferred_element_type=F32)
        for s in range(rep):
            grads[s][:, at] = grad[s * per : (s + 1) * per, :].astype(grads[s].dtype)


def down_kernel(rep, cap, rank, nb, *refs):
    vslot, tokens = refs[:2]
    parts = refs[2 : 2 + rep]
    down, a_all = refs[3 + rep : 5 + rep]
    turned = refs[5 + rep]
    per = cap * rank
    width = a_all.shape[1]
    for s in range(rep):
        a_all[s * per : (s + 1) * per, :] = parts[s][:, :width]
    chunk = 4
    for r in range(nb // chunk):
        prod = lax.dot_general(
            tokens[r * chunk * BLOCK : (r + 1) * chunk * BLOCK, :], a_all[...], NT, preferred_element_type=F32
        )
        for b in range(chunk):
            turned[r * chunk + b] = prod[b * BLOCK : (b + 1) * BLOCK, :].T
    for b in range(nb):
        start = pl.multiple_of(vslot[b] * rank, rank)
        down[:, b * BLOCK : (b + 1) * BLOCK] = turned[b, pl.ds(start, rank), :]


def grad_b_kernel(rep, cap, rank, nb, *refs):
    vslot, down_here, down_there, upstream, near_a = refs[:5]
    grads = refs[5:-1]
    spread = refs[-1]
    per = cap * rank
    cols = grads[0].shape[1]
    at = pl.multiple_of(lax.axis_index("tp") * cols, cols)
    spread[...] = jnp.zeros_like(spread)
    total = (SCALE * (down_here[...] + down_there[...])).astype(BF16)
    for b in range(nb):
        start = pl.multiple_of(vslot[b] * rank, rank)
        spread[pl.ds(start, rank), b * BLOCK : (b + 1) * BLOCK] = total[:, b * BLOCK : (b + 1) * BLOCK]
    grad = jnp.dot(spread[...], upstream[:, pl.ds(at, cols)], preferred_element_type=F32)
    for s in range(rep):
        part = grad[s * per : (s + 1) * per, :].astype(grads[s].dtype)
        if s == 1:
            grads[s][:, : near_a.shape[1]] = near_a[...]
            grads[s][:, near_a.shape[1] :] = part
        else:
            grads[s][...] = part


def token_kernel(chunk, tiles, *refs):
    frozen, up_scaled, a_all = refs[:3]
    out, buf, sems = refs[-3:]
    rows = up_scaled.shape[0]
    pending = {}
    for n, (start, size) in enumerate(tiles):
        slot = n % 2
        cols = slice(start, start + size)
        for r in range(rows // chunk):
            at = slice(r * chunk, (r + 1) * chunk)
            if (slot, r) in pending:
                pending.pop((slot, r)).wait()
            total = jnp.dot(up_scaled[at, :], a_all[:, cols], preferred_element_type=F32)
            total = frozen[at, cols] + total
            buf[slot, at, :size] = total.astype(BF16)
            copy = pltpu.make_async_copy(
                buf.at[slot, pl.ds(r * chunk, chunk), pl.ds(0, size)],
                out.at[pl.ds(r * chunk, chunk), pl.ds(start, size)],
                sems.at[slot, r],
            )
            copy.start()
            pending[slot, r] = copy
    wait_all(pending.values())


def finish_kernel(rep, cap, rank, *refs):
    pick = refs[0]
    far = rep - 2
    near = refs[1 + far]
    own_a, own_b = refs[2 + 2 * far : 4 + 2 * far]
    in_a = (own_a, near, *refs[1 : 1 + far])
    in_b = (own_b, near, *refs[2 + far : 2 + 2 * far])
    out_a, out_b, sum_a, sum_b, sem = refs[1 + 2 * rep :]
    halves = 4
    width = sum_a.shape[2] // halves
    copies = []
    for h in range(halves):
        cols = slice(h * width, (h + 1) * width)
        sum_a[:, :, cols] = jnp.zeros(sum_a.shape[:2] + (width,), F32)
        if h == 0:
            sum_b[...] = jnp.zeros_like(sum_b)
        for s in range(rep):
            for c in range(cap):
                to = pick[s * cap + c]
                at = slice(c * rank, (c + 1) * rank)

                @pl.when(to >= 0)
                def _():
                    sum_a[to, :, cols] += in_a[s][at, cols].astype(F32)
                    if h == 0:
                        sum_b[to] += in_b[s][at, in_b[s].shape[1] - sum_b.shape[2] :].astype(F32)

        part = pl.ds(h * width, width)
        copies.append(pltpu.make_async_copy(sum_a.at[:, :, part], out_a.at[:, :, part], sem.at[h]))
        copies[-1].start()
        if h == 0:
            copies.append(pltpu.make_async_copy(sum_b, out_b, sem.at[halves]))
            copies[-1].start()
    wait_all(copies)


def local(tokens_in, upstream, base_weight, bank_a, bank_b, slot_ids, used_lists):
    rows, width = tokens_in.shape
    outs = upstream.shape[1]
    held, rank, cols = bank_b.shape
    slots = used_lists.shape[1]
    nb = rows // BLOCK
    rep = lax.axis_size("rep")
    tp = lax.axis_size("tp")
    cap = (slots + rep - 1) // rep
    per = cap * rank
    depth = rep * per
    tile = chunk = 512
    tie = lax.optimization_barrier

    def swap(axis, x, s):
        return lax.ppermute(x, axis, [(i, i ^ s) for i in range(lax.axis_size(axis))])

    def bits(n):
        return [1 << i for i in range(n.bit_length() - 1)]

    a_flat = in_hbm(bank_a.reshape(held * rank, width))
    b_flat = in_hbm(bank_b.reshape(held * rank, cols))
    w_flat = in_hbm(base_weight)
    vslot, bank, upstream_v, weight_first, own_list = kernel(
        functools.partial(plan_kernel, cap, held),
        "plan",
        [
            struct((nb,), I32),
            pltpu.VMEM((held * rank, width + cols), BF16),
            pltpu.VMEM((rows, outs), BF16),
            pltpu.VMEM((tile, outs), BF16),
            pltpu.VMEM((1, slots), I32),
        ],
        [HBM] * 6,
        [SMEM] + [VMEM] * 4,
        [
            in_hbm(used_lists),
            in_hbm(slot_ids.reshape(nb, BLOCK)),
            a_flat,
            b_flat,
            in_hbm(upstream),
            w_flat,
        ],
        [
            pltpu.SMEM((1, slots), I32),
            pltpu.SMEM((nb, BLOCK), I32),
            pltpu.SMEM((slots,), I32),
            pltpu.SemaphoreType.DMA((7,)),
        ],
    )

    lists = tie((*[swap("rep", used_lists, s) for s in range(1, rep)], vslot, bank))
    *sends, pick = kernel(
        functools.partial(pick_kernel, rep, cap, held),
        "pick",
        [struct((per, width + cols), BF16)] * rep + [struct((rep * cap,), I32)],
        [ANY] * rep + [VMEM],
        [VMEM] * rep + [SMEM],
        [own_list, *lists[: rep - 1], lists[rep]],
        [pltpu.SMEM((1, slots), I32)] * rep + [pltpu.SemaphoreType.DMA((rep,))],
    )
    vslot = lists[rep - 1]
    fetched = {s: swap("rep", sends[s], s) for s in range(1, rep)}
    fetched[0] = sends[0]

    frozen, tokens_v, upstream_v = kernel(
        functools.partial(frozen_kernel, chunk, tile),
        "frozen",
        [pltpu.VMEM((rows, width), F32), pltpu.VMEM((rows, width), BF16), pltpu.VMEM((rows, outs), BF16)],
        [VMEM, VMEM, HBM, HBM, HBM, ANY],
        [VMEM] * 3,
        [upstream_v, weight_first, w_flat, in_hbm(tokens_in), in_hbm(upstream), sends[0]],
        [
            pltpu.VMEM((width - tile, outs), BF16),
            pltpu.SemaphoreType.DMA((width // tile + rows // chunk,)),
        ],
        {0: 2},
    )
    *far, upstream_v, tokens_v, frozen = tie((*[fetched[s] for s in range(2, rep)], upstream_v, tokens_v, frozen))
    *fetched, upstream_v = tie((fetched[0], fetched[1], *far, upstream_v))

    quarter = jnp.concatenate([x[:, width:] for x in fetched], axis=0)
    down, a_all = kernel(
        functools.partial(down_kernel, rep, cap, rank, nb),
        "down",
        [struct((rank, rows), F32), struct((depth, width), BF16)],
        [SMEM, VMEM] + [VMEM] * rep + [ANY],
        [VMEM, VMEM],
        [vslot, tokens_v, *fetched, quarter],
        [pltpu.VMEM((nb, depth, BLOCK), F32)],
    )
    held_q, came_q, order = quarter, None, [0]
    for bit in bits(tp)[::-1]:
        if came_q is not None:
            held_q = jnp.concatenate([held_q, came_q], axis=0)
            order += [s ^ (2 * bit) for s in order]
        came_q = swap("tp", held_q, bit)
        if bit == tp // 2:
            came_q, down = tie((came_q, down))
    up_first = kernel(
        functools.partial(up_first_kernel, chunk, order),
        "up_first",
        pltpu.VMEM((rows, depth), F32),
        [VMEM] * 2,
        VMEM,
        [upstream_v, held_q],
    )
    for bit in bits(tp)[:-1]:
        came = swap("tp", down, bit)
        if bit == 1:
            came, up_first = tie((came, up_first))
        down = down + came
    down_there = swap("tp", down, tp // 2)

    up_scaled, *grads_a = kernel(
        functools.partial(up_kernel, rep, cap, rank, nb, order),
        "up_grad_a",
        [struct((rows, depth), BF16), struct((per, width), F32)] + [struct((per, width), BF16)] * (rep - 1),
        [SMEM] + [VMEM] * 4 + [ANY],
        [VMEM] * (rep + 1),
        [vslot, upstream_v, up_first, came_q, tokens_v, down],
    )
    grads_b = kernel(
        functools.partial(grad_b_kernel, rep, cap, rank, nb),
        "grad_b",
        [struct((per, cols), F32), struct((per, width + cols), BF16)] + [struct((per, cols), BF16)] * (rep - 2),
        [SMEM] + [VMEM] * 4,
        [VMEM] * rep,
        [vslot, down, down_there, upstream_v, grads_a[1]],
        [pltpu.VMEM((depth, rows), BF16)],
    )
    far_a = [swap("rep", grads_a[s], s) for s in range(2, rep)]
    near = swap("rep", grads_b[1], 1)
    far_b = [swap("rep", grads_b[s], s) for s in range(2, rep)]

    token_gradient = kernel(
        functools.partial(token_kernel, chunk, [(at, tile) for at in range(0, width, tile)]),
        "token_gradient",
        pltpu.HBM((rows, width), BF16),
        [VMEM] * 3 + [ANY],
        HBM,
        [frozen, up_scaled, a_all, grads_b[0]],
        [pltpu.VMEM((2, rows, tile), BF16), pltpu.SemaphoreType.DMA((2, rows // chunk))],
        flops=8 * rows * width * depth,
    )

    grad_a, grad_b = kernel(
        functools.partial(finish_kernel, rep, cap, rank),
        "finish",
        [pltpu.HBM((held, rank, width), F32), pltpu.HBM((held, rank, cols), F32)],
        [SMEM] + [VMEM] * (2 * rep - 1) + [HBM],
        [HBM] * 2,
        [pick, *far_a, near, *far_b, grads_a[0], grads_b[0], in_hbm(token_gradient)],
        [
            pltpu.VMEM((held, rank, width), F32),
            pltpu.VMEM((held, rank, cols), F32),
            pltpu.SemaphoreType.DMA((5,)),
        ],
    )
    return token_gradient, grad_a, grad_b


def solution(mesh):
    in_specs = (
        P(("groups", "rep"), "tp"),
        P(("groups", "rep"), None),
        P("tp", None),
        P("rep", None, "tp"),
        P("rep", None, "tp"),
        P(("groups", "rep")),
        P(("groups", "rep"), None),
    )
    out_specs = (
        P(("groups", "rep"), "tp"),
        P(("groups", "rep"), None, "tp"),
        P(("groups", "rep"), None, "tp"),
    )
    return jax.shard_map(local, mesh=mesh, in_specs=in_specs, out_specs=out_specs, check_vma=False)
```
